32 devices in a mesh: blk: 8 (over y, x, core), docs: 4 (over z).
Axes of the slice: x: 2, y: 2, z: 4, core: 2. Of those that a mesh axis runs over, the one named last changes fastest.
Arguments:
- acts: bfloat16 [16384, 4096], P(('blk', 'docs')), may hold values from -6 to 6
- grads: bfloat16 [16384, 7168], P(('blk', 'docs')), may hold values from -6 to 6
- proj_in: bfloat16 [4096, 64], replicated, may hold values from -0.09375 to 0.09375
- proj_out: bfloat16 [7168, 64], replicated, may hold values from -0.0625 to 0.0625
- doc_ids: int32 [16384], P('blk'), may hold values from 0 to 511, as said below
- doc_slot: int32 [512], replicated, may hold values from 0 to 511, as said below
- train_grads: bfloat16 [32768, 4096], P(('blk', 'docs')), may hold values from -0.09375 to 0.09375
- train_scale: float32 [32768], P(('blk', 'docs')), may hold values from 0.5 to 4
Outputs:
- scores: float32 [512, 32768], P(None, ('blk', 'docs'))
The draws below stay inside these ranges and needn't reach their ends.
Inputs may be any that keep to these rules, and one draw needn't show every extreme that they name: `doc_ids`: tokens of group b (rows b * 2048 to (b + 1) * 2048 - 1) name only documents b * 64 to (b + 1) * 64 - 1; each document is one contiguous run of 16 or more tokens, a multiple of 16 long, and every document is named. `doc_slot`: within each group b, documents b * 64 to (b + 1) * 64 - 1 take the slots b * 64 to (b + 1) * 64 - 1, each once; slot s is owned by docs index (s // 16) % 4.
All inputs are finite; a program needn't handle non-finite values.
Results may differ from the reference program's by a relative error of at most 0.005.
Values may be sent and summed in bfloat16 or wider, within the bound.
A program may use at most 128 MiB of HBM per device.

```python
import math
import jax
import jax.numpy as jnp
from jax import lax

D = 4096
HW = 7168
RANK = 64
GROUP_TOK = 2048
GROUP_DOCS = 64
TOKENS = 16384
QDOCS = 512
NTRAIN = 32768


def group_ids(group_key):
    candidates = GROUP_TOK // 16
    shuffled = jax.random.permutation(group_key, candidates - 1) + 1
    boundaries = jnp.sort(shuffled[:GROUP_DOCS - 1]) * 16
    positions = jnp.arange(GROUP_TOK, dtype=jnp.int32)
    return jnp.sum((boundaries[None, :] <= positions[:, None]).astype(jnp.int32), axis=1)


def draw_doc_ids(key, part):
    group_count = TOKENS // GROUP_TOK
    group_keys = jax.random.split(jax.random.fold_in(key, 11), group_count)
    local_ids = jax.vmap(group_ids)(group_keys)
    offsets = jnp.arange(group_count, dtype=jnp.int32)[:, None] * GROUP_DOCS
    return (local_ids + offsets).reshape(-1).astype(jnp.int32)


def draw_doc_slot(key, part):
    group_count = QDOCS // GROUP_DOCS
    group_keys = jax.random.split(jax.random.fold_in(key, 23), group_count)
    shuffled = jax.vmap(lambda single: jax.random.permutation(single, GROUP_DOCS))(group_keys)
    offsets = jnp.arange(group_count, dtype=jnp.int32)[:, None] * GROUP_DOCS
    return (shuffled + offsets).reshape(-1).astype(jnp.int32)


def block_scale(stream_key, dims, cuts, low, largest):
    factor_of = 1.0
    for position, parts in cuts:
        steps = jax.random.uniform(jax.random.fold_in(jax.random.fold_in(stream_key, 6), position), (parts,), jnp.float32, low / len(cuts), largest / len(cuts))
        factor_of = factor_of * jnp.repeat(jnp.exp(steps), dims[position] // parts).reshape((-1,) + (1,) * (len(dims) - 1 - position))
    return factor_of


def gaussian(own_key, shape, scale, bound, cuts=(), held_as=jnp.bfloat16):
    entries = scale * jax.random.normal(own_key, shape, jnp.float32)
    if cuts:
        entries = entries * block_scale(own_key, shape, cuts, -0.22, 0.18)
    return jnp.clip(entries, -bound, bound).astype(held_as)


def setup_inputs(seed: int = 0) -> dict:
    streams_of = jax.random.split(jax.random.key(seed), 9)
    acts = gaussian(streams_of[0], (TOKENS, D), 1.0, 6.0, ((0, 32),))
    grads = gaussian(streams_of[1], (TOKENS, HW), 1.0, 6.0, ((0, 32),))
    proj_in = gaussian(streams_of[2], (D, RANK), D ** -0.5, 0.09375)
    proj_out = gaussian(streams_of[3], (HW, RANK), HW ** -0.5, 0.0625)
    doc_ids = draw_doc_ids(jax.random.fold_in(streams_of[8], 71), 0)
    doc_slot = draw_doc_slot(jax.random.fold_in(streams_of[8], 71), 0)
    train_grads = gaussian(streams_of[6], (NTRAIN, RANK * RANK), (RANK * RANK) ** -0.5, 0.09375, ((0, 32),))
    train_scale = jnp.clip(jnp.exp(math.log(4.0) - 2.0794415 * jax.random.uniform(streams_of[7], (NTRAIN,), jnp.float32) ** block_scale(streams_of[7], (NTRAIN,), ((0, 32),), -0.2, 0.2)), 0.5, 4.0)
    return {"acts": acts, "grads": grads, "proj_in": proj_in, "proj_out": proj_out, "doc_ids": doc_ids, "doc_slot": doc_slot, "train_grads": train_grads, "train_scale": train_scale}


def group_blocks(inputs):
    left_rows, right_rows, slots = inputs
    owners = (slots[:, None] == jnp.arange(GROUP_DOCS, dtype=jnp.int32)[None, :]).astype(jnp.bfloat16)
    weighted = (owners[:, :, None] * right_rows[:, None, :]).reshape(GROUP_TOK, GROUP_DOCS * RANK)
    blocks = lax.dot_general(weighted, left_rows, (((0,), (0,)), ((), ())), preferred_element_type=jnp.float32)
    return blocks.reshape(GROUP_DOCS, RANK * RANK).astype(jnp.bfloat16)


def reference(acts, grads, proj_in, proj_out, doc_ids, doc_slot, train_grads, train_scale):
    left_rows = jnp.dot(acts, proj_in, preferred_element_type=jnp.float32).astype(jnp.bfloat16)
    right_rows = jnp.dot(grads, proj_out, preferred_element_type=jnp.float32).astype(jnp.bfloat16)
    slots = (jnp.take(doc_slot, doc_ids) % GROUP_DOCS).astype(jnp.int32)
    group_count = TOKENS // GROUP_TOK
    docgrad = lax.map(group_blocks, (left_rows.reshape(group_count, GROUP_TOK, RANK), right_rows.reshape(group_count, GROUP_TOK, RANK), slots.reshape(group_count, GROUP_TOK)))
    docgrad = docgrad.reshape(QDOCS, RANK * RANK)
    scores = lax.dot_general(docgrad, train_grads, (((1,), (1,)), ((), ())), preferred_element_type=jnp.float32)
    return scores * train_scale[None, :]
```

```python
import functools

import jax
import jax.numpy as jnp
from jax import lax
from jax.experimental import pallas as pl
from jax.experimental.pallas import tpu as pltpu
from jax.sharding import PartitionSpec as P

RUN = 16
CLS = 4
PARTS = 2
F32 = jnp.float32
BF16 = jnp.bfloat16


def flip(value, step):
    return value + (1 - 2 * ((value // step) % 2)) * step


def xor(a, b, bits):
    return sum(((((a // (1 << k)) % 2) + ((b // (1 << k)) % 2)) % 2) * (1 << k) for k in range(bits))


def kernel(nb, nq, group_docs, acts, grads, pin, pout, slots, train, out,
           a_v, g_v, t_v, rt_v, gat, blocks, prod, mask_l, load_sem, t_sem, send_sem, recv_sem):
    b, d = lax.axis_index("blk"), lax.axis_index("docs")
    chip, core = b // 2, b % 2
    chips = nb // 2
    bits = chips.bit_length() - 1
    tok = acts.shape[0]
    width = pin.shape[1]
    half = tok // 2
    pairs = width // 2
    nd = tok // RUN // CLS
    part = tok // PARTS

    loads = []
    for p in range(PARTS):
        rows = pl.ds(p * part, part)
        loads.append((
            pltpu.make_async_copy(acts.at[rows], a_v.at[rows], load_sem.at[2 * p]),
            pltpu.make_async_copy(grads.at[rows], g_v.at[rows], load_sem.at[2 * p + 1]),
        ))
    for one, two in loads:
        one.start()
        two.start()
    t_copy = pltpu.make_async_copy(train, t_v, t_sem)
    t_copy.start()

    sibling = (flip(b, 1), d)
    partners = [(flip(b, 2 << k), d) for k in range(bits)]
    peers = [(b, lax.rem(d + k, nq)) for k in range(1, nq)]
    barrier = pltpu.get_barrier_semaphore()
    for who in [sibling] + partners + peers:
        pl.semaphore_signal(barrier, inc=1, device_id=who, device_id_type=pl.DeviceIdType.MESH)

    t_id = lax.broadcasted_iota(jnp.int32, (tok, CLS * width), 0)
    l_id = lax.broadcasted_iota(jnp.int32, (tok, CLS * width), 1)
    cls, at = (t_id // RUN) % CLS, l_id // width
    mask_l[0] = (cls == at).astype(F32).astype(BF16)
    swapped = at + 1 - 2 * (at % 2)
    mask_l[1] = (cls == swapped).astype(F32).astype(BF16)

    lefts = []
    for p in range(PARTS):
        rows = pl.ds(p * part, part)
        loads[p][0].wait()
        lefts.append(jnp.dot(a_v[rows, :], pin[...], preferred_element_type=F32))
        loads[p][1].wait()
        right = jnp.dot(g_v[rows, :], pout[...], preferred_element_type=F32)
        turned = right.T
        for tb in range(part // 128):
            rt_v[pl.ds((p * part // 128 + tb) * width, width), :] = turned[:, tb * 128:(tb + 1) * 128]
    left = jnp.concatenate(lefts, axis=0)
    gat[0, 0, 0, pl.ds(0, half), :] = jnp.concatenate([left[:half], left[half:]], axis=1).astype(BF16)
    tiles = tok // 128
    for h in range(2):
        for tb in range(tiles):
            rows = rt_v[pl.ds(tb * width + h, pairs, stride=2), :].astype(BF16)
            gat[0, 0, 0, pl.ds(half + (h * tiles + tb) * pairs, pairs), :] = rows
    gat[0, 0, 0, pl.ds(tok, 16), :] = slots[...]

    pl.semaphore_wait(barrier, 1 + bits + nq - 1)

    sends = []

    def send(src, dst, who):
        index = len(sends)
        copy = pltpu.make_async_remote_copy(
            src_ref=gat.at[src], dst_ref=gat.at[dst],
            send_sem=send_sem.at[index], recv_sem=recv_sem.at[dst],
            device_id=who, device_id_type=pl.DeviceIdType.MESH)
        copy.start()
        sends.append(copy)

    def arrived(slot):
        pltpu.make_async_remote_copy(
            src_ref=gat.at[slot], dst_ref=gat.at[slot],
            send_sem=send_sem.at[0], recv_sem=recv_sem.at[slot],
            device_id=sibling, device_id_type=pl.DeviceIdType.MESH).wait_recv()

    def order(j):
        return list(range(bits)) if j % 2 == 0 else list(range(bits))[::-1]

    def spread(j, stage):
        o = order(j)
        if stage == 0:
            new = [0]
            if j:
                arrived((j, 0, 0))
        else:
            new = [0]
            for k in range(stage - 1):
                new = new + [r + (1 << o[k]) for r in new]
            new = [r + (1 << o[stage - 1]) for r in new]
            for r in new:
                arrived((j, r, 0))
        for k in range(stage, bits):
            for r in new:
                send((j, r, 0), (j, r + (1 << o[k]), 0), partners[o[k]])
        for r in new:
            send((j, r, 0), (j, r, 1), sibling)

    def first(j):
        spread(j, 0)

    def rest(j):
        for stage in range(1, bits + 1):
            spread(j, stage)
        for r in range(chips):
            arrived((j, r, 1))

    low = lax.broadcasted_iota(jnp.int32, (half, 2 * width), 1) < width
    low_p = lax.broadcasted_iota(jnp.int32, (pairs * nd, 2 * width), 1) < width
    d_id = lax.broadcasted_iota(jnp.int32, (nd, tok), 0)
    mask_d = (d_id == lax.broadcasted_iota(jnp.int32, (nd, tok), 1) // (RUN * CLS)).astype(F32)

    def outer(j):
        def pair(r, carry):
            results = []
            for a in range(2):
                slot = gat.at[j, r, lax.rem(core + a, 2)]
                packed = slot[pl.ds(0, half), :].astype(F32)
                turned = pltpu.roll(packed, width, 1)
                dup = jnp.concatenate([jnp.where(low, packed, turned), jnp.where(low, turned, packed)], axis=0).astype(BF16)
                wide = jnp.concatenate([dup] * (CLS // 2), axis=1)
                parts = []
                for h in range(2):
                    rt = jnp.concatenate(
                        [slot[pl.ds(half + (h * tiles + tb) * pairs, pairs), :] for tb in range(tiles)], axis=1).astype(F32)
                    lhs = (rt[:, None, :] * mask_d[None, :, :]).reshape(pairs * nd, tok).astype(BF16)
                    parts.append(jnp.dot(lhs, wide * mask_l[h], preferred_element_type=F32))
                results.append(parts)
            base = xor(chip, r, bits) * (2 * nd * CLS)
            for ch in range(CLS // 2):
                cols = slice(ch * 2 * width, (ch + 1) * 2 * width)
                for cl in range(2):
                    pieces = []
                    for a in range(2):
                        e, f = results[a][0][:, cols], results[a][1][:, cols]
                        if cl == 0:
                            pieces.append(jnp.where(low_p, e, f))
                        else:
                            pieces.append(pltpu.roll(jnp.where(low_p, f, e), width, 1))
                    at_row = pl.multiple_of(base + (ch * 2 + cl) * 2 * nd, 16)
                    for p in range(pairs):
                        rows = slice(p * nd, (p + 1) * nd)
                        tile = jnp.concatenate([pieces[0][rows], pieces[1][rows]], axis=0)
                        blocks[pl.ds(at_row, 2 * nd), pl.ds(p * 2 * width, 2 * width)] = tile.astype(BF16)
            return carry
        lax.fori_loop(0, chips, pair, 0)

    def finish(j):
        n_tile = 256
        four = 4 * group_docs
        per = 4 * nd * CLS

        def tile(n, carry):
            cols = pl.ds(pl.multiple_of(n * n_tile, n_tile), n_tile)
            prod[...] = lax.dot_general(blocks[...], t_v[cols, :], (((1,), (1,)), ((), ())), preferred_element_type=F32)

            def put(q4, c2):
                vec = jnp.zeros((1, 128), F32)
                for s in range(2):
                    r = xor(chip, q4 * 2 + s, bits)
                    for a in range(2):
                        vec = vec + gat[j, r, a, pl.ds(tok, 16), :].astype(F32)[0:1]
                lane = lax.broadcasted_iota(jnp.int32, (1, 128), 1)
                group = 2 * (lane // 64) + (lane % 16) // 8
                target = vec + (group * group_docs).astype(F32)
                row = lax.broadcasted_iota(jnp.int32, (four, 128), 0).astype(F32)
                pick = (row == target).astype(F32).astype(BF16)
                x = prod[pl.ds(pl.multiple_of(q4 * per, per), per), :]
                hi = x.astype(BF16)
                lo = (x - hi.astype(F32)).astype(BF16)
                add = jnp.dot(pick, hi, preferred_element_type=F32) + jnp.dot(pick, lo, preferred_element_type=F32)
                rows = pl.ds(pl.multiple_of(q4 * four, four), four)
                if j == 0:
                    out[rows, cols] = add
                else:
                    out[rows, cols] += add
                return c2
            return lax.fori_loop(0, chips // 2, put, carry)
        lax.fori_loop(0, train.shape[0] // n_tile, tile, 0)

    for k in range(1, nq):
        send((0, 0, 0), (k, 0, 0), peers[k - 1])
    first(0)
    for j in range(nq):
        if j + 1 < nq:
            first(j + 1)
        rest(j)
        outer(j)
        if j == 0:
            t_copy.wait()
        finish(j)
    for copy in sends:
        copy.wait_send()


def body(acts, grads, proj_in, proj_out, doc_ids, doc_slot, train_grads, train_scale):
    nb, nq = lax.axis_size("blk"), lax.axis_size("docs")
    b, d = lax.axis_index("blk"), lax.axis_index("docs")
    tok, width = acts.shape[0], proj_in.shape[1]
    docs = doc_slot.shape[0]
    group_docs = docs // nb
    chips = nb // 2
    bits = chips.bit_length() - 1
    nd = tok // RUN // CLS

    own = lax.dynamic_slice(doc_slot, (b * group_docs,), (group_docs,)) % group_docs
    ids = lax.dynamic_slice(doc_ids.reshape(-1, tok // RUN, RUN)[:, :, 0], (d, 0), (1, tok // RUN))[0] - b * group_docs
    ids = jnp.transpose(ids.reshape(nd, CLS)).reshape(CLS, 1, nd)
    found = jnp.sum(jnp.where(ids[..., None] == jnp.arange(group_docs), own, 0), axis=-1)
    here = ((jnp.arange(2)[:, None, None, None] == (b // 2) % 2) & (jnp.arange(2)[None, None, :, None] == b % 2))
    vec = jnp.where(here, found[None], 0).reshape(1, 4 * nd * CLS).astype(BF16)
    slots = jnp.broadcast_to(vec, (16, vec.shape[1]))

    rows = tok + 16
    n_sends = nq - 1 + nq * (chips - 1 + chips)
    any_spec = pl.BlockSpec(memory_space=pl.ANY)
    vmem = pl.BlockSpec(memory_space=pltpu.VMEM)
    product = pl.pallas_call(
        functools.partial(kernel, nb, nq, group_docs),
        out_shape=jax.ShapeDtypeStruct((docs, train_grads.shape[0]), F32),
        in_specs=[any_spec, any_spec, vmem, vmem, vmem, any_spec],
        out_specs=vmem,
        scratch_shapes=[
            pltpu.VMEM(acts.shape, BF16),
            pltpu.VMEM(grads.shape, BF16),
            pltpu.VMEM(train_grads.shape, BF16),
            pltpu.VMEM((tok // 128 * width, 128), F32),
            pltpu.VMEM((nq, chips, 2, rows, 128), BF16),
            pltpu.VMEM((nb * nd * CLS, width * width), BF16),
            pltpu.VMEM((nb * nd * CLS, 256), F32),
            pltpu.VMEM((2, tok, CLS * width), BF16),
            pltpu.SemaphoreType.DMA((2 * PARTS,)),
            pltpu.SemaphoreType.DMA,
            pltpu.SemaphoreType.DMA((n_sends,)),
            pltpu.SemaphoreType.DMA((nq, chips, 2)),
        ],
        compiler_params=pltpu.CompilerParams(
            collective_id=0, has_side_effects=True, vmem_limit_bytes=62 * 2**20),
        cost_estimate=pl.CostEstimate(flops=10**10, bytes_accessed=25 * 10**6, transcendentals=0),
    )(acts, grads, proj_in, proj_out, slots, train_grads)
    return product * train_scale[None, :]


def solution(mesh):
    placed = (
        P(("blk", "docs"), None),
        P(("blk", "docs"), None),
        P(),
        P(),
        P("blk"),
        P(),
        P(("blk", "docs"), None),
        P(("blk", "docs")),
    )
    return jax.shard_map(
        body, mesh=mesh, in_specs=placed, out_specs=P(None, ("blk", "docs")), check_vma=False
    )
```
